128 devices in a mesh: ctx: 32 (over y_hi, x, z), head: 4 (over y_lo, core).
Axes of the slice: x: 4, y: 4 (y_hi: 2, y_lo: 2; y = y_hi * 2 + y_lo), z: 4, core: 2. Of those that a mesh axis runs over, the one named last changes fastest.
Arguments:
- query: bfloat16 [8192, 3072], P(('ctx', 'head')), may hold values from -8 to 8
- key: bfloat16 [8192, 512], P(('ctx', 'head')), may hold values from -8 to 8
- value: bfloat16 [8192, 512], P(('ctx', 'head')), may hold values from -24 to 24
- residual: bfloat16 [8192, 6144], P(('ctx', 'head')), may hold values from -4 to 4
- out_weight: bfloat16 [3072, 6144], P('head'), may hold values from -0.109375 to 0.109375
- gate_table: float32 [4, 6144], replicated, may hold values from 0.5 to 2
- span_of_shard: int32 [32], replicated, may hold values from 0 to 3, as said below
- noise_level: int32 [4], replicated, may hold values from 0 to 3
- visible: int32 [4, 4], replicated, may hold values from 0 to 1, as said below
Outputs:
- mixed: bfloat16 [8192, 6144], P(('ctx', 'head'))
The draws below stay inside these ranges and needn't reach their ends.
Inputs may be any that keep to these rules, and one draw needn't show every extreme that they name: `span_of_shard`: Non-decreasing along the shards, starts at 0, ends at 3, and every span holds at least one shard. `visible`: the diagonal is 1 and every entry above it is 0.
All inputs are finite; a program needn't handle non-finite values.
Results may differ from the reference program's by a relative error of at most 0.015.
Values may be sent and summed in bfloat16 or wider, within the bound.
A program may use at most 64 MiB of HBM per device.

```python
import math
import jax
import jax.numpy as jnp
from jax import lax

D = 6144
HEADS = 24
KV_HEADS = 4
HD = 128
SPANS = 4
LEVELS = 4
TOKENS = 8192
N_CTX = 32


def draw_query(key, part):
    key = jax.random.fold_in(key, 11)
    base = jnp.clip(1.4 * jax.random.normal(key, (TOKENS, HEADS * HD), jnp.float32), -8.0, 8.0)
    return base.astype(jnp.bfloat16)


def draw_key(key, part):
    key = jax.random.fold_in(key, 23)
    base = jnp.clip(1.4 * jax.random.normal(key, (TOKENS, KV_HEADS * HD), jnp.float32), -8.0, 8.0)
    return base.astype(jnp.bfloat16)


def draw_span_of_shard(key, part):
    key = jax.random.fold_in(key, 37)
    order = jax.random.permutation(key, N_CTX - 1)
    cuts = order[:SPANS - 1].astype(jnp.int32) + 1
    shards = jnp.arange(N_CTX, dtype=jnp.int32)
    return jnp.sum((shards[:, None] >= cuts[None, :]).astype(jnp.int32), axis=1).astype(jnp.int32)


def draw_visible(key, part):
    key = jax.random.fold_in(key, 41)
    coins = jax.random.bernoulli(key, 0.6, (SPANS, SPANS)).astype(jnp.int32)
    rows = jnp.arange(SPANS, dtype=jnp.int32)[:, None]
    cols = jnp.arange(SPANS, dtype=jnp.int32)[None, :]
    table = jnp.where(rows > cols, coins, 0)
    return jnp.where(rows == cols, 1, table).astype(jnp.int32)


def touch_ends(values, rng, smallest, high):
    longest = values.shape.index(max(values.shape))
    spots = []
    for shift in (0, 1):
        where = [jax.random.randint(jax.random.fold_in(rng, axis), (), 0, length) for axis, length in enumerate(values.shape)]
        where[longest] = (where[longest] + shift) % values.shape[longest]
        spots.append(tuple(where))
    return values.at[spots[0]].set(smallest).at[spots[1]].set(high)


def level_of(own_key, dims, cuts, smallest, top_value):
    loudness, own = 1.0, jax.random.fold_in(own_key, 6)
    for dim, shards_of in cuts:
        heights = jnp.exp(jax.random.uniform(jax.random.fold_in(own, dim), (shards_of,), jnp.float32, smallest / len(cuts), top_value / len(cuts)))
        loudness = loudness * jnp.repeat(heights, dims[dim] // shards_of).reshape([-1 if axis == dim else 1 for axis in range(len(dims))])
    return loudness


def bell_draw(rng, extent, deviation, bound, pieces=(), kind=jnp.bfloat16):
    gain = level_of(rng, extent, pieces, -0.22, 0.18) if pieces else 1.0
    entries = jax.random.normal(rng, extent, jnp.float32) * deviation * gain
    return jnp.minimum(jnp.maximum(entries, -bound), bound).astype(kind)


def setup_inputs(seed: int = 0) -> dict:
    streams_of = jax.random.split(jax.random.key(seed), 10)
    query = draw_query(jax.random.fold_in(streams_of[9], 71), 0)
    key = draw_key(jax.random.fold_in(streams_of[9], 71), 0)
    value = bell_draw(streams_of[2], (TOKENS, KV_HEADS * HD), 4.0, 24.0, ((0, 128),))
    residual = bell_draw(streams_of[3], (TOKENS, D), 0.5, 4.0, ((0, 128),))
    out_weight = bell_draw(streams_of[4], (HEADS * HD, D), (HEADS * HD) ** -0.5, 0.109375, ((0, 4),))
    gate_table = jnp.clip(jax.random.uniform(streams_of[5], (LEVELS, D), jnp.float32, 0.5, 2.0), 0.5, 2.0)
    span_of_shard = draw_span_of_shard(jax.random.fold_in(streams_of[9], 71), 0)
    noise_level = touch_ends(jax.random.randint(streams_of[7], (SPANS,), 0, LEVELS), jax.random.fold_in(streams_of[7], 1), 0, LEVELS - 1).astype(jnp.int32)
    visible = draw_visible(jax.random.fold_in(streams_of[9], 71), 0)
    return {"query": query, "key": key, "value": value, "residual": residual, "out_weight": out_weight, "gate_table": gate_table, "span_of_shard": span_of_shard, "noise_level": noise_level, "visible": visible}


NEG = -1e+30

def reference(query, key, value, residual, out_weight, gate_table, span_of_shard, noise_level, visible):
    tokens = query.shape[0]
    tok_ctx = tokens // N_CTX
    share = HEADS // KV_HEADS
    token_span = jnp.repeat(span_of_shard, tok_ctx, total_repeat_length=tokens).astype(jnp.int32)
    vis_rows = visible[token_span].astype(jnp.float32)
    block = math.gcd(tokens, 512)
    scale = 1.0 / math.sqrt(HD)
    q_heads = query.reshape(tokens, KV_HEADS, share, HD).transpose(1, 2, 0, 3)
    k_heads = key.reshape(tokens, KV_HEADS, HD).transpose(1, 0, 2)
    v_heads = value.reshape(tokens, KV_HEADS, HD).transpose(1, 0, 2)

    def one_head(operands):
        q_g, k_h, v_h = operands
        k_f = k_h.astype(jnp.float32)
        v_f = v_h.astype(jnp.float32)

        def one_block(index):
            start = (index * block).astype(jnp.int32)
            q_b = lax.dynamic_slice_in_dim(q_g, start, block, 1).astype(jnp.float32)
            rows_vis = lax.dynamic_slice_in_dim(vis_rows, start, block, 0)
            allowed = (rows_vis[:, token_span] > 0.5)[None]
            scores = jnp.einsum('gqd,kd->gqk', q_b, k_f) * scale
            masked = jnp.where(allowed, scores, NEG)
            top = lax.optimization_barrier(jnp.max(masked, axis=2, keepdims=True))
            weights = jnp.where(allowed, jnp.exp(masked - top), 0.0)
            total = lax.optimization_barrier(jnp.sum(weights, axis=2))
            rounded = lax.optimization_barrier(weights.astype(jnp.bfloat16)).astype(jnp.float32)
            numer = jnp.einsum('gqk,kd->gqd', rounded, v_f)
            return (numer / total[:, :, None]).astype(jnp.bfloat16)
        result = lax.map(one_block, jnp.arange(tokens // block, dtype=jnp.int32))
        return result.transpose(1, 0, 2, 3).reshape(share, tokens, HD)
    attended = lax.map(one_head, (q_heads, k_heads, v_heads))
    attended = attended.transpose(2, 0, 1, 3).reshape(tokens, HEADS * HD)
    projected = jnp.dot(attended, out_weight, preferred_element_type=jnp.float32)
    gate = gate_table[noise_level[token_span]]
    return (residual.astype(jnp.float32) + gate * projected).astype(jnp.bfloat16)
```

```python
import math

import jax
import jax.numpy as jnp
from jax import lax
from jax.experimental import pallas as pl
from jax.experimental.pallas import tpu as pltpu
from jax.sharding import PartitionSpec as P

HD = 128
KV_HEADS = 4
SHARE = 6
WIDTH = SHARE * HD
BLOCK = 64
ROWS = SHARE * BLOCK
D = 6144
CHUNKS = 6
CHUNK = D // CHUNKS
RING = 4
NEG = -1e30
BIG = 1e30
MESH = pl.DeviceIdType.MESH

PLACE = {
    (0, 0): 0,
    (1, 0): 1,
    (0, 1): 2,
    (3, 0): 3,
    (0, 3): 4,
    (1, 1): 5,
    (3, 3): 6,
    (3, 1): 7,
    (1, 3): 8,
    (2, 0): 9,
    (0, 2): 10,
    (2, 1): 11,
    (1, 2): 12,
    (2, 3): 13,
    (3, 2): 14,
    (2, 2): 15,
}
COLUMNS = len(PLACE)
STEPS = COLUMNS // 2
ARRIVE = {
    0: [(1, 0), (3, 0), (0, 1), (0, 3)],
    1: [(1, 1), (2, 0)],
    2: [(3, 3), (3, 1), (1, 3)],
    3: [(0, 2)],
    4: [(2, 1), (2, 3), (1, 2)],
    5: [(3, 2)],
    6: [(2, 2)],
}


def layer_kernel(
    query,
    key,
    value,
    residual,
    weight,
    gate_table,
    span_of_shard,
    noise_level,
    visible,
    out,
    kv,
    q_in,
    q_rows,
    top,
    acc,
    att_out,
    att,
    w_here,
    res_here,
    gate_here,
    part_out,
    part_in,
    part_keep,
    cross_out,
    cross_in,
    mask,
    local_sem,
    k_send,
    k_recv,
    v_send,
    v_recv,
    q_send,
    q_recv,
    g_send,
    g_recv,
    s_send,
    s_recv,
    a_send,
    a_recv,
    p_send,
    p_recv,
    c_send,
    c_recv,
):
    ctx = lax.axis_index("ctx")
    head = lax.axis_index("head")
    y_hi, x, z = ctx // 16, (ctx // 4) % 4, ctx % 4
    y_lo, core = head // 2, head % 2
    y = y_hi * 2 + y_lo
    other = 1 - core

    def device(y_at, x_at, z_at, core_at):
        return ((y_at // 2) * 16 + x_at * 4 + z_at, (y_at % 2) * 2 + core_at)

    def in_column(step, core_at):
        return device((y + step) % 4, x, z, core_at)

    sibling = in_column(0, other)

    def along(axis, step):
        on_x = (1 - core) if axis == 0 else core
        return device(y, (x + on_x * (step + 4)) % 4, (z + (1 - on_x) * (step + 4)) % 4, core)

    def place(first, second):
        a, b = PLACE[(first, second)], PLACE[(second, first)]
        return a if a == b else a + core * (b - a)

    def remote(src, dst, send, recv, to):
        return pltpu.make_async_remote_copy(
            src_ref=src, dst_ref=dst, send_sem=send, recv_sem=recv, device_id=to, device_id_type=MESH
        )

    local = [
        pltpu.make_async_copy(weight, w_here, local_sem.at[0]),
        pltpu.make_async_copy(residual, res_here, local_sem.at[1]),
        pltpu.make_async_copy(gate_table, gate_here, local_sem.at[2]),
    ]

    barrier = pltpu.get_barrier_semaphore()
    peers = [in_column(1, core), in_column(2, core), in_column(3, core)]
    peers += [sibling, in_column(2, other)]
    peers += [along(0, 1), along(0, -1), along(1, 1), along(1, -1)]
    for peer in peers:
        pl.semaphore_signal(barrier, inc=1, device_id=peer, device_id_type=MESH)
    pl.semaphore_wait(barrier, len(peers))

    key_rows = pl.ds(pl.multiple_of(y_lo * BLOCK, BLOCK), BLOCK)

    def key_copy(step, which):
        chip = (y + step) % 4
        group = (chip % 2) * 2 + chip // 2
        src = (key, value)[which].at[:, pl.ds(pl.multiple_of(group * HD, HD), HD)]
        dst = kv.at[0, core, y_hi, which, key_rows]
        send, recv = ((k_send, k_recv), (v_send, v_recv))[which]
        if step == 0:
            return pltpu.make_async_copy(src, dst, recv.at[0])
        return remote(src, dst, send.at[step], recv.at[step], in_column(step, core))

    def query_copy(step):
        chip = (y + step) % 4
        group = (chip % 2) * 2 + chip // 2
        src = query.at[:, pl.ds(pl.multiple_of(group * WIDTH, WIDTH), WIDTH)]
        block = {0: 3, 1: 1 - core, 2: 2, 3: core}[step]
        dst = q_in.at[block]
        if step == 0:
            return pltpu.make_async_copy(src, dst, q_recv.at[0])
        return remote(src, dst, q_send.at[step], q_recv.at[step], in_column(step, core))

    for step in (2, 1, 3, 0):
        for which in range(2):
            key_copy(step, which).start()
    for step in (1, 3, 2, 0):
        query_copy(step).start()
    for copy in local:
        copy.start()

    span_here = [span_of_shard[x * 4 + z], span_of_shard[16 + x * 4 + z]]
    for (dx, dz), at in PLACE.items():
        column = ((x + 4 - dx) % 4) * 4 + (z + 4 - dz) % 4
        for half in range(2):
            span = span_of_shard[half * 16 + column]
            for row in range(2):
                mask[row, at * 2 + half] = visible[span_here[row], span]

    top[...] = jnp.full(top.shape, NEG, jnp.float32)
    acc[...] = jnp.zeros(acc.shape, jnp.float32)

    def full_copy(first, second, axis, step):
        src = kv.at[place(first, second), core]
        there = ((first + step) % 4, second) if axis == 0 else (first, (second + step) % 4)
        at = place(*there)
        return remote(src, kv.at[at, core], g_send.at[at, 0], g_recv.at[at, 0], along(axis, step))

    def half_copy(first, second, axis, step):
        half = 0 if step == 1 else 1
        src = kv.at[place(first, second), core, half]
        there = ((first + step) % 4, second) if axis == 0 else (first, (second + step) % 4)
        at = place(*there)
        return remote(
            src, kv.at[at, core, half], g_send.at[at, half], g_recv.at[at, half], along(axis, step)
        )

    def side_copy(at):
        return remote(kv.at[at, core], kv.at[at, core], s_send.at[at], s_recv.at[at], sibling)

    def side_wait(at):
        remote(kv.at[at, other], kv.at[at, other], s_send.at[at], s_recv.at[at], sibling).wait_recv()

    def onward(first, second):
        copies = []
        if second == 0:
            if first == 0:
                copies += [full_copy(0, 0, 0, 1), full_copy(0, 0, 0, -1)]
            if first == 1:
                copies += [half_copy(1, 0, 0, 1)]
            if first == 3:
                copies += [half_copy(3, 0, 0, -1)]
            copies += [full_copy(first, 0, 1, 1), full_copy(first, 0, 1, -1)]
        elif second == 1:
            copies += [half_copy(first, 1, 1, 1)]
        elif second == 3:
            copies += [half_copy(first, 3, 1, -1)]
        return copies + [side_copy(place(first, second))]

    def arrive(first, second):
        at = place(first, second)
        if (second if second else first) == 2:
            for half in range(2):
                spot = kv.at[at, core, half]
                remote(spot, spot, g_send.at[at, half], g_recv.at[at, half], sibling).wait_recv()
        else:
            spot = kv.at[at, core]
            remote(spot, spot, g_send.at[at, 0], g_recv.at[at, 0], sibling).wait_recv()
        for copy in onward(first, second):
            copy.start()

    for step in range(4):
        for which in range(2):
            copy = key_copy(step, which)
            if step == 0:
                copy.wait()
            else:
                copy.wait_recv()
    for copy in onward(0, 0):
        copy.start()
    for offset in ARRIVE[0]:
        arrive(*offset)

    scale = math.log2(math.e) / math.sqrt(HD)

    def take_queries(block):
        for one in range(SHARE):
            rows = q_in[block, :, one * HD : (one + 1) * HD].astype(jnp.float32) * scale
            upper = rows.astype(jnp.bfloat16)
            lower = (rows - upper.astype(jnp.float32)).astype(jnp.bfloat16)
            spot = pl.ds(block * ROWS + one * BLOCK, BLOCK)
            q_rows[spot, :HD] = upper
            q_rows[spot, HD:] = lower

    def block_chip(block):
        step = [1 + core * 2, 3 - core * 2, 2, 0][block]
        return (y + step) % 4

    def attend(blocks, i):
        groups = [(2 * i + late, half) for late in range(2) for half in range(2)]
        spots = [(at, side, half) for at, half in groups for side in range(2)]
        keys = jnp.concatenate([kv[at, side, half, 0] for at, side, half in spots], axis=0)
        keys = jnp.concatenate([keys, keys], axis=1)
        values = jnp.concatenate([kv[at, side, half, 1] for at, side, half in spots], axis=0)
        values = jnp.concatenate([values, jnp.ones_like(values)], axis=1)
        scores = [
            lax.dot_general(
                q_rows[block * ROWS : (block + 1) * ROWS],
                keys,
                (((1,), (1,)), ((), ())),
                preferred_element_type=jnp.float32,
            )
            for block in blocks
        ]
        ready = []
        for block, score in zip(blocks, scores):
            rows = slice(block * ROWS, (block + 1) * ROWS)
            shard = block_chip(block) // 2
            seen = [mask[shard, at * 2 + half] > 0 for at, half in groups]
            parts = [score[:, n * 2 * HD : (n + 1) * 2 * HD] for n in range(len(groups))]
            best = None
            for part, ok in zip(parts, seen):
                most = jnp.where(ok, jnp.maximum(part[:, :HD], part[:, HD:]), NEG)
                best = most if best is None else jnp.maximum(best, most)
            old = top[rows]
            new = jnp.maximum(old, jnp.max(best, axis=1, keepdims=True))
            top[rows] = new
            weights = [
                jnp.exp2(part - jnp.where(ok, new, BIG)).astype(jnp.bfloat16)
                for part, ok in zip(parts, seen)
            ]
            ready.append((rows, jnp.concatenate(weights, axis=1), jnp.exp2(old - new)))
        for rows, weights, factor in ready:
            acc[rows] = acc[rows] * factor + jnp.dot(
                weights, values, preferred_element_type=jnp.float32
            )

    def far_copy(phase, block):
        src = att_out.at[block]
        dst = att.at[phase, pl.ds(pl.multiple_of(core * BLOCK, BLOCK), BLOCK)]
        return remote(
            src, dst, a_send.at[phase, 0], a_recv.at[phase, core], in_column(2, y_hi)
        )

    def near_copy(phase, block, stays):
        src = att_out.at[block]
        dst = att.at[phase, pl.ds(pl.multiple_of(core * BLOCK, BLOCK), BLOCK)]
        if stays:
            return pltpu.make_async_copy(src, dst, a_recv.at[phase, core])
        return remote(src, dst, a_send.at[phase, 1], a_recv.at[phase, core], sibling)

    def send_attended(phase):
        for block in (2 * phase, 2 * phase + 1):
            rows = slice(block * ROWS, (block + 1) * ROWS)
            attended = (acc[rows, :HD] / acc[rows, HD:]).astype(jnp.bfloat16)
            for one in range(SHARE):
                att_out[block, :, one * HD : (one + 1) * HD] = attended[
                    one * BLOCK : (one + 1) * BLOCK
                ]
        far_copy(phase, 2 * phase).start()

        @pl.when(core == y_hi)
        def _():
            near_copy(phase, 2 * phase + 1, True).start()

        @pl.when(core != y_hi)
        def _():
            near_copy(phase, 2 * phase + 1, False).start()

    def part_copy(phase, n):
        return remote(
            part_out.at[phase, n],
            part_in.at[phase, n],
            p_send.at[phase, n],
            p_recv.at[phase, n],
            sibling,
        )

    def cross_copy(n):
        return remote(
            cross_out.at[n],
            cross_in.at[n],
            c_send.at[n],
            c_recv.at[n],
            in_column(3 - 2 * core, core),
        )

    def project(phase):
        for side in range(2):
            spot = att.at[phase, side * BLOCK : (side + 1) * BLOCK]
            remote(spot, spot, a_send.at[phase, 0], a_recv.at[phase, side], sibling).wait_recv()
        rows = att[phase]
        for n in range(CHUNKS):
            part = jnp.dot(
                rows,
                w_here[:, n * CHUNK : (n + 1) * CHUNK],
                preferred_element_type=jnp.float32,
            )
            first, second = part[:BLOCK], part[BLOCK:]
            part_out[phase, n] = jnp.where(core == 0, second, first).astype(jnp.bfloat16)
            part_copy(phase, n).start()
            part_keep[n] = jnp.where(core == 0, first, second)

    def cross_send():
        for n in range(CHUNKS):
            part_copy(0, n).wait_recv()
            total = part_keep[n] + part_in[0, n].astype(jnp.float32)
            cross_out[n] = total.astype(jnp.bfloat16)
            cross_copy(n).start()

    query_copy(1).wait_recv()
    query_copy(3).wait_recv()
    take_queries(0)
    take_queries(1)

    def early(i, carry):
        for at in ARRIVE:
            if at:

                @pl.when(i == at)
                def _(at=at):
                    for offset in ARRIVE[at]:
                        arrive(*offset)

        @pl.when(i > 0)
        def _():
            side_wait(2 * i)

        side_wait(2 * i + 1)
        attend((0, 1), i)
        return carry

    side_wait(0)
    lax.fori_loop(0, STEPS, early, 0)
    send_attended(0)
    local[0].wait()

    query_copy(0).wait()
    query_copy(2).wait_recv()
    take_queries(2)
    take_queries(3)

    def late(i, carry):
        attend((2, 3), i)

        @pl.when(i == 1)
        def _():
            project(0)

        @pl.when(i == 3)
        def _():
            cross_send()

        return carry

    lax.fori_loop(0, STEPS, late, 0)
    send_attended(1)
    local[1].wait()
    local[2].wait()
    level = noise_level[span_here[0] * (1 - y_hi) + span_here[1] * y_hi]
    project(1)
    for n in range(CHUNKS):
        columns = slice(n * CHUNK, (n + 1) * CHUNK)
        gate = jnp.zeros((1, CHUNK), jnp.float32)
        for at in range(gate_here.shape[0]):
            gate = jnp.where(level == at, gate_here[at : at + 1, columns], gate)
        part_copy(1, n).wait_recv()
        cross_copy(n).wait_recv()
        total = part_keep[n] + part_in[1, n].astype(jnp.float32) + cross_in[n].astype(jnp.float32)
        out[:, columns] = (res_here[:, columns].astype(jnp.float32) + gate * total).astype(
            jnp.bfloat16
        )

    for step in (1, 2, 3):
        key_copy(step, 0).wait_send()
        key_copy(step, 1).wait_send()
        query_copy(step).wait_send()
    for first in range(4):
        for second in range(4):
            for copy in onward(first, second):
                copy.wait_send()
    for phase in range(2):
        far_copy(phase, 2 * phase).wait_send()

        @pl.when(core != y_hi)
        def _(phase=phase):
            near_copy(phase, 2 * phase + 1, False).wait_send()

        for n in range(CHUNKS):
            part_copy(phase, n).wait_send()
    for n in range(CHUNKS):
        cross_copy(n).wait_send()


def on_device(*arrays):
    anywhere = pl.BlockSpec(memory_space=pl.ANY)
    scalars = pl.BlockSpec(memory_space=pltpu.SMEM)
    bf16, f32 = jnp.bfloat16, jnp.float32
    dma = pltpu.SemaphoreType.DMA
    return pl.pallas_call(
        layer_kernel,
        out_shape=jax.ShapeDtypeStruct((BLOCK, D), bf16),
        in_specs=[anywhere] * 6 + [scalars] * 3,
        out_specs=pl.BlockSpec(memory_space=pltpu.VMEM),
        scratch_shapes=[
            pltpu.VMEM((COLUMNS, 2, 2, 2, HD, HD), bf16),
            pltpu.VMEM((4, BLOCK, WIDTH), bf16),
            pltpu.VMEM((4 * ROWS, 2 * HD), bf16),
            pltpu.VMEM((4 * ROWS, 1), f32),
            pltpu.VMEM((4 * ROWS, 2 * HD), f32),
            pltpu.VMEM((4, BLOCK, WIDTH), bf16),
            pltpu.VMEM((2, 2 * BLOCK, WIDTH), bf16),
            pltpu.VMEM((WIDTH, D), bf16),
            pltpu.VMEM((BLOCK, D), bf16),
            pltpu.VMEM((4, D), f32),
            pltpu.VMEM((2, CHUNKS, BLOCK, CHUNK), bf16),
            pltpu.VMEM((2, CHUNKS, BLOCK, CHUNK), bf16),
            pltpu.VMEM((CHUNKS, BLOCK, CHUNK), f32),
            pltpu.VMEM((CHUNKS, BLOCK, CHUNK), bf16),
            pltpu.VMEM((CHUNKS, BLOCK, CHUNK), bf16),
            pltpu.SMEM((2, 2 * COLUMNS), jnp.int32),
            dma((3,)),
            dma((4,)),
            dma((4,)),
            dma((4,)),
            dma((4,)),
            dma((4,)),
            dma((4,)),
            dma((COLUMNS, 2)),
            dma((COLUMNS, 2)),
            dma((COLUMNS,)),
            dma((COLUMNS,)),
            dma((2, 2)),
            dma((2, 2)),
            dma((2, CHUNKS)),
            dma((2, CHUNKS)),
            dma((CHUNKS,)),
            dma((CHUNKS,)),
        ],
        compiler_params=pltpu.CompilerParams(
            collective_id=0, has_side_effects=True, vmem_limit_bytes=58 * 2**20
        ),
        name="span_attention_layer",
    )(*arrays)


def solution(mesh):
    tokens = P(("ctx", "head"), None)
    placed = (tokens, tokens, tokens, tokens, P("head", None), P(), P(), P(), P())
    return jax.shard_map(
        on_device, mesh=mesh, in_specs=placed, out_specs=tokens, check_vma=False
    )
```

```python
import math

import jax
import jax.numpy as jnp
from jax import lax
from jax.experimental import pallas as pl
from jax.experimental.pallas import tpu as pltpu
from jax.sharding import PartitionSpec as P

HD = 128
KV_HEADS = 4
SHARE = 6
WIDTH = SHARE * HD
BLOCK = 64
ROWS = SHARE * BLOCK
D = 6144
CHUNKS = 6
CHUNK = D // CHUNKS
RING = 4
NEG = -1e30
BIG = 1e30
MESH = pl.DeviceIdType.MESH

PLACE = {
    (0, 0): 0,
    (1, 0): 1,
    (0, 1): 2,
    (3, 0): 3,
    (0, 3): 4,
    (1, 1): 5,
    (3, 3): 6,
    (3, 1): 7,
    (1, 3): 8,
    (2, 0): 9,
    (0, 2): 10,
    (2, 1): 11,
    (1, 2): 12,
    (2, 3): 13,
    (3, 2): 14,
    (2, 2): 15,
}
COLUMNS = len(PLACE)
STEPS = COLUMNS // 2
FILL = {1: (0, 1)}
AHEAD = 1
LEFT = STEPS - AHEAD
LAG = 4
FIRST = [(1, 0), (3, 0), (0, 1), (0, 3)]
ARRIVE = {
    1: [(1, 1), (3, 3), (3, 1), (1, 3), (0, 2)],
    3: [(2, 1), (2, 3)],
    5: [(2, 2)],
}
MIDDLE = {
    0: [(2, 0)],
    3: [(1, 2), (3, 2)],
}


def layer_kernel(
    query,
    key,
    value,
    residual,
    weight,
    gate_table,
    span_of_shard,
    noise_level,
    visible,
    out,
    kv,
    q_in,
    q_rows,
    top,
    acc,
    score_a,
    score_b,
    weight_a,
    weight_b,
    factor_a,
    factor_b,
    score_c,
    score_d,
    weight_c,
    weight_d,
    factor_c,
    factor_d,
    att_out,
    att,
    w_here,
    res_here,
    gate_here,
    part_out,
    part_in,
    part_keep,
    cross_out,
    cross_in,
    mask,
    q_own,
    k_own,
    v_own,
    local_sem,
    k_send,
    k_recv,
    v_send,
    v_recv,
    q_send,
    q_recv,
    g_send,
    g_recv,
    s_send,
    s_recv,
    a_send,
    a_recv,
    p_send,
    p_recv,
    c_send,
    c_recv,
    o_sem,
):
    ctx = lax.axis_index("ctx")
    head = lax.axis_index("head")
    y_hi, x, z = ctx // 16, (ctx // 4) % 4, ctx % 4
    y_lo, core = head // 2, head % 2
    y = y_hi * 2 + y_lo
    other = 1 - core

    def device(y_at, x_at, z_at, core_at):
        return ((y_at // 2) * 16 + x_at * 4 + z_at, (y_at % 2) * 2 + core_at)

    def in_column(step, core_at):
        return device((y + step) % 4, x, z, core_at)

    sibling = in_column(0, other)

    def along(axis, step):
        on_x = (1 - core) if axis == 0 else core
        return device(y, (x + on_x * (step + 4)) % 4, (z + (1 - on_x) * (step + 4)) % 4, core)

    def place(first, second):
        a, b = PLACE[(first, second)], PLACE[(second, first)]
        return a if a == b else a + core * (b - a)

    def remote(src, dst, send, recv, to):
        return pltpu.make_async_remote_copy(
            src_ref=src, dst_ref=dst, send_sem=send, recv_sem=recv, device_id=to, device_id_type=MESH
        )

    local = [
        pltpu.make_async_copy(weight, w_here, local_sem.at[0]),
        pltpu.make_async_copy(residual, res_here, local_sem.at[1]),
        pltpu.make_async_copy(gate_table, gate_here, local_sem.at[2]),
    ]

    own = [
        pltpu.make_async_copy(key, k_own, local_sem.at[3]),
        pltpu.make_async_copy(value, v_own, local_sem.at[4]),
        pltpu.make_async_copy(query, q_own, local_sem.at[5]),
    ]
    for copy in own:
        copy.start()

    barrier = pltpu.get_barrier_semaphore()
    peers = [in_column(1, core), in_column(2, core), in_column(3, core)]
    peers += [sibling, in_column(2, other)]
    peers += [along(0, 1), along(0, -1), along(1, 1), along(1, -1)]
    for peer in peers:
        pl.semaphore_signal(barrier, inc=1, device_id=peer, device_id_type=MESH)
    top[...] = jnp.full(top.shape, NEG, jnp.float32)
    acc[...] = jnp.zeros(acc.shape, jnp.float32)
    for copy in own:
        copy.wait()
    pl.semaphore_wait(barrier, len(peers))

    key_rows = pl.ds(pl.multiple_of(y_lo * BLOCK, BLOCK), BLOCK)

    def key_copy(step, which):
        chip = (y + step) % 4
        group = (chip % 2) * 2 + chip // 2
        src = (k_own, v_own)[which].at[:, pl.ds(pl.multiple_of(group * HD, HD), HD)]
        dst = kv.at[0, core, y_hi, which, key_rows]
        send, recv = ((k_send, k_recv), (v_send, v_recv))[which]
        if step == 0:
            return pltpu.make_async_copy(src, dst, recv.at[0])
        return remote(src, dst, send.at[step], recv.at[step], in_column(step, core))

    def query_copy(step):
        chip = (y + step) % 4
        group = (chip % 2) * 2 + chip // 2
        src = q_own.at[:, pl.ds(pl.multiple_of(group * WIDTH, WIDTH), WIDTH)]
        block = {0: 3, 1: 1 - core, 2: 2, 3: core}[step]
        dst = q_in.at[block]
        if step == 0:
            return pltpu.make_async_copy(src, dst, q_recv.at[0])
        return remote(src, dst, q_send.at[step], q_recv.at[step], in_column(step, core))

    for step in (2, 1, 3, 0):
        for which in range(2):
            key_copy(step, which).start()
    for step in (1, 3, 0):
        query_copy(step).start()
    for copy in local:
        copy.start()

    span_here = [span_of_shard[x * 4 + z], span_of_shard[16 + x * 4 + z]]
    for (dx, dz), at in PLACE.items():
        column = ((x + 4 - dx) % 4) * 4 + (z + 4 - dz) % 4
        for half in range(2):
            span = span_of_shard[half * 16 + column]
            for row in range(2):
                mask[row, at * 2 + half] = visible[span_here[row], span]

    def ring_copy(first, second, axis, step, half):
        there = ((first + step) % 4, second) if axis == 0 else (first, (second + step) % 4)
        at = place(*there)
        if half is None:
            src, dst, n = kv.at[place(first, second), core], kv.at[at, core], 0
        else:
            src, dst, n = kv.at[place(first, second), core, half], kv.at[at, core, half], half
        return remote(src, dst, g_send.at[at, n], g_recv.at[at, n], along(axis, step))

    def side_copy(at):
        return remote(kv.at[at, core], kv.at[at, core], s_send.at[at], s_recv.at[at], sibling)

    def side_wait(at):
        remote(kv.at[at, other], kv.at[at, other], s_send.at[at], s_recv.at[at], sibling).wait_recv()

    def onward(first, second):
        ways = []
        if second == 0:
            if first == 0:
                ways += [(0, 1, None), (0, -1, None)]
            if first == 1:
                ways += [(0, 1, 0)]
            if first == 3:
                ways += [(0, -1, 1)]
            ways += [(1, 1, None), (1, -1, None)]
        elif second == 1:
            ways += [(1, 1, 0)]
        elif second == 3:
            ways += [(1, -1, 1)]
        return [ring_copy(first, second, *way) for way in ways]

    def arrive(first, second):
        at = place(first, second)
        if (second if second else first) == 2:
            for half in range(2):
                spot = kv.at[at, core, half]
                remote(spot, spot, g_send.at[at, half], g_recv.at[at, half], sibling).wait_recv()
        else:
            spot = kv.at[at, core]
            remote(spot, spot, g_send.at[at, 0], g_recv.at[at, 0], sibling).wait_recv()
        for copy in onward(first, second):
            copy.start()
        side_copy(at).start()

    for step in range(4):
        for which in range(2):
            copy = key_copy(step, which)
            if step == 0:
                copy.wait()
            else:
                copy.wait_recv()
    for copy in onward(0, 0):
        copy.start()
    side_copy(0).start()
    weight_a[...] = jnp.zeros(weight_a.shape, jnp.bfloat16)
    weight_b[...] = jnp.zeros(weight_b.shape, jnp.bfloat16)
    factor_a[...] = jnp.ones(factor_a.shape, jnp.float32)
    factor_b[...] = jnp.ones(factor_b.shape, jnp.float32)
    for offset in FIRST:
        arrive(*offset)

    scale = math.log2(math.e) / math.sqrt(HD)

    def take_queries(block):
        for one in range(SHARE):
            rows = q_in[block, :, one * HD : (one + 1) * HD].astype(jnp.float32) * scale
            upper = rows.astype(jnp.bfloat16)
            lower = (rows - upper.astype(jnp.float32)).astype(jnp.bfloat16)
            spot = pl.ds(block * ROWS + one * BLOCK, BLOCK)
            q_rows[spot, :HD] = upper
            q_rows[spot, HD:] = lower

    def rows_of(block):
        if isinstance(block, int):
            return pl.ds(block * ROWS, ROWS)
        return pl.ds(pl.multiple_of(block * ROWS, ROWS), ROWS)

    def groups_of(pair):
        return [(2 * pair + late, half) for late in range(2) for half in range(2)]

    def both_sides(pair, which):
        return jnp.concatenate(
            [kv[at, side, half, which] for at, half in groups_of(pair) for side in range(2)], axis=0
        )

    scores = (score_a, score_b, score_c, score_d)
    weights = (weight_a, weight_b, weight_c, weight_d)
    factors = (factor_a, factor_b, factor_c, factor_d)

    def score(block, pair, slot):
        keys = both_sides(pair, 0)
        keys = jnp.concatenate([keys, keys], axis=1)
        scores[slot][...] = lax.dot_general(
            q_rows[rows_of(block)],
            keys,
            (((1,), (1,)), ((), ())),
            preferred_element_type=jnp.float32,
        )

    def weigh(block, shard, pair, slot):
        rows = rows_of(block)
        groups = groups_of(pair)
        seen = [mask[shard, at * 2 + half] > 0 for at, half in groups]
        parts = [scores[slot][:, n * 2 * HD : (n + 1) * 2 * HD] for n in range(len(groups))]
        best = None
        for part, ok in zip(parts, seen):
            most = jnp.where(ok, jnp.maximum(part[:, :HD], part[:, HD:]), NEG)
            best = most if best is None else jnp.maximum(best, most)
        old = top[rows]
        new = jnp.maximum(old, jnp.max(best, axis=1, keepdims=True))
        top[rows] = new
        for n, (part, ok) in enumerate(zip(parts, seen)):
            weights[slot][:, n * 2 * HD : (n + 1) * 2 * HD] = jnp.exp2(
                part - jnp.where(ok, new, BIG)
            ).astype(jnp.bfloat16)
        factors[slot][...] = jnp.exp2(old - new)

    def gather(block, pair, slot):
        rows = rows_of(block)
        values = both_sides(pair, 1)
        values = jnp.concatenate([values, jnp.ones_like(values)], axis=1)
        acc[rows] = acc[rows] * factors[slot][...] + jnp.dot(
            weights[slot][...], values, preferred_element_type=jnp.float32
        )

    def shard_at(step):
        return ((y + step) % 4) // 2

    def far_copy(phase, block):
        src = att_out.at[block]
        dst = att.at[phase, pl.ds(pl.multiple_of(core * BLOCK, BLOCK), BLOCK)]
        return remote(
            src, dst, a_send.at[phase, 0], a_recv.at[phase, core], in_column(2, y_hi)
        )

    def near_copy(phase, block, stays):
        src = att_out.at[block]
        dst = att.at[phase, pl.ds(pl.multiple_of(core * BLOCK, BLOCK), BLOCK)]
        if stays:
            return pltpu.make_async_copy(src, dst, a_recv.at[phase, core])
        return remote(src, dst, a_send.at[phase, 1], a_recv.at[phase, core], sibling)

    def normalise(block):
        rows = rows_of(block)
        attended = (acc[rows, :HD] / acc[rows, HD:]).astype(jnp.bfloat16)
        for one in range(SHARE):
            att_out[block, :, one * HD : (one + 1) * HD] = attended[one * BLOCK : (one + 1) * BLOCK]

    def send_far(phase):
        normalise(2 * phase)
        far_copy(phase, 2 * phase).start()

    def send_near(phase):
        normalise(2 * phase + 1)

        @pl.when(core == y_hi)
        def _():
            near_copy(phase, 2 * phase + 1, True).start()

        @pl.when(core != y_hi)
        def _():
            near_copy(phase, 2 * phase + 1, False).start()

    def part_copy(phase, n):
        return remote(
            part_out.at[phase, n],
            part_in.at[phase, n],
            p_send.at[phase, n],
            p_recv.at[phase, n],
            sibling,
        )

    def cross_copy(n):
        return remote(
            cross_out.at[n],
            cross_in.at[n],
            c_send.at[n],
            c_recv.at[n],
            in_column(3 - 2 * core, core),
        )

    def cross_send(n):
        part_copy(0, n).wait_recv()
        total = part_keep[n] + part_in[0, n].astype(jnp.float32)
        cross_out[n] = total.astype(jnp.bfloat16)
        cross_copy(n).start()

    def out_copy(n):
        columns = pl.ds(n * CHUNK, CHUNK)
        return pltpu.make_async_copy(res_here.at[:, columns], out.at[:, columns], o_sem.at[n])

    level = noise_level[span_here[0] * (1 - y_hi) + span_here[1] * y_hi]

    def finish(n):
        columns = slice(n * CHUNK, (n + 1) * CHUNK)
        gate = jnp.zeros((1, CHUNK), jnp.float32)
        for at in range(gate_here.shape[0]):
            gate = jnp.where(level == at, gate_here[at : at + 1, columns], gate)
        part_copy(1, n).wait_recv()
        cross_copy(n).wait_recv()
        total = part_keep[n] + part_in[1, n].astype(jnp.float32) + cross_in[n].astype(jnp.float32)
        res_here[:, columns] = (res_here[:, columns].astype(jnp.float32) + gate * total).astype(
            jnp.bfloat16
        )
        out_copy(n).start()

    def project(phase, use):
        for side in range(2):
            spot = att.at[phase, side * BLOCK : (side + 1) * BLOCK]
            remote(spot, spot, a_send.at[phase, 0], a_recv.at[phase, side], sibling).wait_recv()
        rows = att[phase]
        for n in range(CHUNKS + LAG):
            if n < CHUNKS:
                part = jnp.dot(
                    rows,
                    w_here[:, n * CHUNK : (n + 1) * CHUNK],
                    preferred_element_type=jnp.float32,
                )
                first, second = part[:BLOCK], part[BLOCK:]
                part_out[phase, n] = jnp.where(core == 0, second, first).astype(jnp.bfloat16)
                part_copy(phase, n).start()
                part_keep[n] = jnp.where(core == 0, first, second)
            if n >= LAG:
                use(n - LAG)

    query_copy(1).wait_recv()
    query_copy(3).wait_recv()
    query_copy(2).start()
    take_queries(0)
    take_queries(1)
    side_wait(0)
    side_wait(1)
    score(0, 0, 0)
    last = STEPS - 1

    def ahead(pair, carry):
        for block in (2, 3):
            score(block, pair, block)
        for block in (2, 3):
            weigh(block, shard_at(6 - 2 * block), pair, block)
        for block in (2, 3):
            gather(block, pair, block)
        return carry

    def early(i, carry):
        @pl.when(i == 1)
        def _():
            query_copy(0).wait()
            query_copy(2).wait_recv()
            take_queries(2)
            take_queries(3)

        for at, (low, high) in FILL.items():

            @pl.when(i == at)
            def _(low=low, high=high):
                lax.fori_loop(low, high, ahead, 0)

        for at in ARRIVE:

            @pl.when(i == at)
            def _(at=at):
                for offset in ARRIVE[at]:
                    arrive(*offset)

        gather(1, jnp.maximum(i - 1, 0), 1)
        score(1, i, 1)
        weigh(0, shard_at(1 + 2 * core), i, 0)
        for at in MIDDLE:

            @pl.when(i == at)
            def _(at=at):
                for offset in MIDDLE[at]:
                    arrive(*offset)

        @pl.when(i < last)
        def _():
            side_wait(2 * i + 2)
            side_wait(2 * i + 3)

        gather(0, i, 0)
        score(jnp.where(i == last, 2, 0), jnp.where(i == last, AHEAD, i + 1), 0)
        weigh(1, shard_at(3 - 2 * core), i, 1)
        return carry

    lax.fori_loop(0, STEPS, early, 0)
    send_far(0)
    local[0].wait()

    def block_of(n):
        return 2 + n // LEFT

    def pair_of(n):
        return AHEAD + n % LEFT

    def late(i, carry):
        n = 2 * i
        gather(
            jnp.where(i == 0, 1, block_of(jnp.maximum(n - 1, 0))),
            jnp.where(i == 0, last, pair_of(jnp.maximum(n - 1, 0))),
            1,
        )
        score(block_of(n + 1), pair_of(n + 1), 1)
        weigh(block_of(n), shard_at(6 - 2 * block_of(n)), pair_of(n), 0)
        gather(block_of(n), pair_of(n), 0)
        score(jnp.minimum(block_of(n + 2), 3), pair_of(n + 2), 0)
        weigh(block_of(n + 1), shard_at(6 - 2 * block_of(n + 1)), pair_of(n + 1), 1)

        @pl.when(i == 0)
        def _():
            send_near(0)

        @pl.when(i == LEFT // 2)
        def _():
            send_far(1)
            project(0, cross_send)

        return carry

    lax.fori_loop(0, LEFT, late, 0)
    gather(3, last, 1)
    send_near(1)
    local[1].wait()
    local[2].wait()
    project(1, finish)
    for n in range(CHUNKS):
        out_copy(n).wait()

    for step in (1, 2, 3):
        key_copy(step, 0).wait_send()
        key_copy(step, 1).wait_send()
        query_copy(step).wait_send()
    for first in range(4):
        for second in range(4):
            for copy in onward(first, second):
                copy.wait_send()
            side_copy(place(first, second)).wait_send()
    for phase in range(2):
        far_copy(phase, 2 * phase).wait_send()

        @pl.when(core != y_hi)
        def _(phase=phase):
            near_copy(phase, 2 * phase + 1, False).wait_send()

        for n in range(CHUNKS):
            part_copy(phase, n).wait_send()
    for n in range(CHUNKS):
        cross_copy(n).wait_send()


def on_device(*arrays):
    anywhere = pl.BlockSpec(memory_space=pl.ANY)
    scalars = pl.BlockSpec(memory_space=pltpu.SMEM)
    bf16, f32 = jnp.bfloat16, jnp.float32
    dma = pltpu.SemaphoreType.DMA
    return pl.pallas_call(
        layer_kernel,
        out_shape=jax.ShapeDtypeStruct((BLOCK, D), bf16),
        in_specs=[anywhere] * 6 + [scalars] * 3,
        out_specs=anywhere,
        scratch_shapes=[
            pltpu.VMEM((COLUMNS, 2, 2, 2, HD, HD), bf16),
            pltpu.VMEM((4, BLOCK, WIDTH), bf16),
            pltpu.VMEM((4 * ROWS, 2 * HD), bf16),
            pltpu.VMEM((4 * ROWS, 1), f32),
            pltpu.VMEM((4 * ROWS, 2 * HD), f32),
            pltpu.VMEM((ROWS, 8 * HD), f32),
            pltpu.VMEM((ROWS, 8 * HD), f32),
            pltpu.VMEM((ROWS, 8 * HD), bf16),
            pltpu.VMEM((ROWS, 8 * HD), bf16),
            pltpu.VMEM((ROWS, 1), f32),
            pltpu.VMEM((ROWS, 1), f32),
            pltpu.VMEM((ROWS, 8 * HD), f32),
            pltpu.VMEM((ROWS, 8 * HD), f32),
            pltpu.VMEM((ROWS, 8 * HD), bf16),
            pltpu.VMEM((ROWS, 8 * HD), bf16),
            pltpu.VMEM((ROWS, 1), f32),
            pltpu.VMEM((ROWS, 1), f32),
            pltpu.VMEM((4, BLOCK, WIDTH), bf16),
            pltpu.VMEM((2, 2 * BLOCK, WIDTH), bf16),
            pltpu.VMEM((WIDTH, D), bf16),
            pltpu.VMEM((BLOCK, D), bf16),
            pltpu.VMEM((4, D), f32),
            pltpu.VMEM((2, CHUNKS, BLOCK, CHUNK), bf16),
            pltpu.VMEM((2, CHUNKS, BLOCK, CHUNK), bf16),
            pltpu.VMEM((CHUNKS, BLOCK, CHUNK), f32),
            pltpu.VMEM((CHUNKS, BLOCK, CHUNK), bf16),
            pltpu.VMEM((CHUNKS, BLOCK, CHUNK), bf16),
            pltpu.SMEM((2, 2 * COLUMNS), jnp.int32),
            pltpu.VMEM((BLOCK, KV_HEADS * WIDTH), bf16),
            pltpu.VMEM((BLOCK, KV_HEADS * HD), bf16),
            pltpu.VMEM((BLOCK, KV_HEADS * HD), bf16),
            dma((6,)),
            dma((4,)),
            dma((4,)),
            dma((4,)),
            dma((4,)),
            dma((4,)),
            dma((4,)),
            dma((COLUMNS, 2)),
            dma((COLUMNS, 2)),
            dma((COLUMNS,)),
            dma((COLUMNS,)),
            dma((2, 2)),
            dma((2, 2)),
            dma((2, CHUNKS)),
            dma((2, CHUNKS)),
            dma((CHUNKS,)),
            dma((CHUNKS,)),
            dma((CHUNKS,)),
        ],
        compiler_params=pltpu.CompilerParams(
            collective_id=0, has_side_effects=True, vmem_limit_bytes=58 * 2**20
        ),
        name="span_attention_layer",
    )(*arrays)


def solution(mesh):
    tokens = P(("ctx", "head"), None)
    placed = (tokens, tokens, tokens, tokens, P("head", None), P(), P(), P(), P())
    return jax.shard_map(
        on_device, mesh=mesh, in_specs=placed, out_specs=tokens, check_vma=False
    )
```

```python
import math

import jax
import jax.numpy as jnp
from jax import lax
from jax.experimental import pallas as pl
from jax.experimental.pallas import tpu as pltpu
from jax.sharding import PartitionSpec as P

HD = 128
KV_HEADS = 4
SHARE = 6
WIDTH = SHARE * HD
BLOCK = 64
ROWS = SHARE * BLOCK
D = 6144
CHUNKS = 6
CHUNK = D // CHUNKS
RING = 4
NEG = -1e30
BIG = 1e30
MESH = pl.DeviceIdType.MESH

PLACE = {
    (0, 0): 0,
    (1, 0): 1,
    (0, 1): 2,
    (3, 0): 3,
    (0, 3): 4,
    (1, 1): 5,
    (3, 3): 6,
    (3, 1): 7,
    (1, 3): 8,
    (2, 0): 9,
    (0, 2): 10,
    (2, 1): 11,
    (1, 2): 12,
    (2, 3): 13,
    (3, 2): 14,
    (2, 2): 15,
}
COLUMNS = len(PLACE)
STEPS = COLUMNS // 2
FILL = {0: (0, 1), 1: (1, 2)}
AHEAD = 2
LEFT = STEPS - AHEAD
LAG = 4
FIRST = [(1, 0), (3, 0), (0, 1), (0, 3)]
ARRIVE = {
    1: [(1, 1), (3, 3), (3, 1), (1, 3), (0, 2)],
    3: [(2, 1), (2, 3)],
    5: [(2, 2)],
}
MIDDLE = {
    0: [(2, 0)],
    3: [(1, 2), (3, 2)],
}


def layer_kernel(
    query,
    key,
    value,
    residual,
    weight,
    gate_table,
    span_of_shard,
    noise_level,
    visible,
    out,
    kv,
    q_in,
    q_rows,
    top,
    acc,
    score_a,
    score_b,
    weight_a,
    weight_b,
    factor_a,
    factor_b,
    score_c,
    score_d,
    weight_c,
    weight_d,
    factor_c,
    factor_d,
    att_out,
    att,
    w_here,
    res_here,
    gate_here,
    part_out,
    part_in,
    part_keep,
    cross_out,
    cross_in,
    mask,
    q_own,
    k_own,
    v_own,
    local_sem,
    k_send,
    k_recv,
    v_send,
    v_recv,
    q_send,
    q_recv,
    g_send,
    g_recv,
    s_send,
    s_recv,
    a_send,
    a_recv,
    p_send,
    p_recv,
    c_send,
    c_recv,
    o_sem,
):
    ctx = lax.axis_index("ctx")
    head = lax.axis_index("head")
    y_hi, x, z = ctx // 16, (ctx // 4) % 4, ctx % 4
    y_lo, core = head // 2, head % 2
    y = y_hi * 2 + y_lo
    other = 1 - core

    def device(y_at, x_at, z_at, core_at):
        return ((y_at // 2) * 16 + x_at * 4 + z_at, (y_at % 2) * 2 + core_at)

    def in_column(step, core_at):
        return device((y + step) % 4, x, z, core_at)

    sibling = in_column(0, other)

    def along(axis, step):
        on_x = (1 - core) if axis == 0 else core
        return device(y, (x + on_x * (step + 4)) % 4, (z + (1 - on_x) * (step + 4)) % 4, core)

    def place(first, second):
        a, b = PLACE[(first, second)], PLACE[(second, first)]
        return a if a == b else a + core * (b - a)

    def remote(src, dst, send, recv, to):
        return pltpu.make_async_remote_copy(
            src_ref=src, dst_ref=dst, send_sem=send, recv_sem=recv, device_id=to, device_id_type=MESH
        )

    local = [
        pltpu.make_async_copy(weight, w_here, local_sem.at[0]),
        pltpu.make_async_copy(residual, res_here, local_sem.at[1]),
        pltpu.make_async_copy(gate_table, gate_here, local_sem.at[2]),
    ]

    own = [
        pltpu.make_async_copy(key, k_own, local_sem.at[3]),
        pltpu.make_async_copy(value, v_own, local_sem.at[4]),
        pltpu.make_async_copy(query, q_own, local_sem.at[5]),
    ]
    for copy in own:
        copy.start()

    barrier = pltpu.get_barrier_semaphore()
    peers = [in_column(1, core), in_column(2, core), in_column(3, core)]
    peers += [sibling, in_column(2, other)]
    peers += [along(0, 1), along(0, -1), along(1, 1), along(1, -1)]
    for peer in peers:
        pl.semaphore_signal(barrier, inc=1, device_id=peer, device_id_type=MESH)
    top[...] = jnp.full(top.shape, NEG, jnp.float32)
    acc[...] = jnp.zeros(acc.shape, jnp.float32)
    for copy in own:
        copy.wait()
    pl.semaphore_wait(barrier, len(peers))

    key_rows = pl.ds(pl.multiple_of(y_lo * BLOCK, BLOCK), BLOCK)

    def key_copy(step, which):
        chip = (y + step) % 4
        group = (chip % 2) * 2 + chip // 2
        src = (k_own, v_own)[which].at[:, pl.ds(pl.multiple_of(group * HD, HD), HD)]
        dst = kv.at[0, core, y_hi, which, key_rows]
        send, recv = ((k_send, k_recv), (v_send, v_recv))[which]
        if step == 0:
            return pltpu.make_async_copy(src, dst, recv.at[0])
        return remote(src, dst, send.at[step], recv.at[step], in_column(step, core))

    def query_copy(step):
        chip = (y + step) % 4
        group = (chip % 2) * 2 + chip // 2
        src = q_own.at[:, pl.ds(pl.multiple_of(group * WIDTH, WIDTH), WIDTH)]
        block = {0: 3, 1: 1 - core, 2: 2, 3: core}[step]
        dst = q_in.at[block]
        if step == 0:
            return pltpu.make_async_copy(src, dst, q_recv.at[0])
        return remote(src, dst, q_send.at[step], q_recv.at[step], in_column(step, core))

    for step in (2, 1, 3, 0):
        for which in range(2):
            key_copy(step, which).start()
    for step in (1, 3, 2, 0):
        query_copy(step).start()
    for copy in local:
        copy.start()

    span_here = [span_of_shard[x * 4 + z], span_of_shard[16 + x * 4 + z]]
    for (dx, dz), at in PLACE.items():
        column = ((x + 4 - dx) % 4) * 4 + (z + 4 - dz) % 4
        for half in range(2):
            span = span_of_shard[half * 16 + column]
            for row in range(2):
                mask[row, at * 2 + half] = visible[span_here[row], span]

    def ring_copy(first, second, axis, step, half):
        there = ((first + step) % 4, second) if axis == 0 else (first, (second + step) % 4)
        at = place(*there)
        if half is None:
            src, dst, n = kv.at[place(first, second), core], kv.at[at, core], 0
        else:
            src, dst, n = kv.at[place(first, second), core, half], kv.at[at, core, half], half
        return remote(src, dst, g_send.at[at, n], g_recv.at[at, n], along(axis, step))

    def side_copy(at):
        return remote(kv.at[at, core], kv.at[at, core], s_send.at[at], s_recv.at[at], sibling)

    def side_wait(at):
        remote(kv.at[at, other], kv.at[at, other], s_send.at[at], s_recv.at[at], sibling).wait_recv()

    def onward(first, second):
        ways = []
        if second == 0:
            if first == 0:
                ways += [(0, 1, None), (0, -1, None)]
            if first == 1:
                ways += [(0, 1, 0)]
            if first == 3:
                ways += [(0, -1, 1)]
            ways += [(1, 1, None), (1, -1, None)]
        elif second == 1:
            ways += [(1, 1, 0)]
        elif second == 3:
            ways += [(1, -1, 1)]
        return [ring_copy(first, second, *way) for way in ways]

    def arrive(first, second):
        at = place(first, second)
        if (second if second else first) == 2:
            for half in range(2):
                spot = kv.at[at, core, half]
                remote(spot, spot, g_send.at[at, half], g_recv.at[at, half], sibling).wait_recv()
        else:
            spot = kv.at[at, core]
            remote(spot, spot, g_send.at[at, 0], g_recv.at[at, 0], sibling).wait_recv()
        for copy in onward(first, second):
            copy.start()
        side_copy(at).start()

    for step in range(4):
        for which in range(2):
            copy = key_copy(step, which)
            if step == 0:
                copy.wait()
            else:
                copy.wait_recv()
    for copy in onward(0, 0):
        copy.start()
    side_copy(0).start()
    weight_a[...] = jnp.zeros(weight_a.shape, jnp.bfloat16)
    weight_b[...] = jnp.zeros(weight_b.shape, jnp.bfloat16)
    factor_a[...] = jnp.ones(factor_a.shape, jnp.float32)
    factor_b[...] = jnp.ones(factor_b.shape, jnp.float32)
    scale = math.log2(math.e) / math.sqrt(HD)

    def take_queries(block):
        for one in range(SHARE):
            rows = q_in[block, :, one * HD : (one + 1) * HD].astype(jnp.float32) * scale
            upper = rows.astype(jnp.bfloat16)
            lower = (rows - upper.astype(jnp.float32)).astype(jnp.bfloat16)
            spot = pl.ds(block * ROWS + one * BLOCK, BLOCK)
            q_rows[spot, :HD] = upper
            q_rows[spot, HD:] = lower

    def rows_of(block):
        if isinstance(block, int):
            return pl.ds(block * ROWS, ROWS)
        return pl.ds(pl.multiple_of(block * ROWS, ROWS), ROWS)

    def groups_of(pair):
        return [(2 * pair + late, half) for late in range(2) for half in range(2)]

    def both_sides(pair, which):
        return jnp.concatenate(
            [kv[at, side, half, which] for at, half in groups_of(pair) for side in range(2)], axis=0
        )

    scores = (score_a, score_b, score_c, score_d)
    weights = (weight_a, weight_b, weight_c, weight_d)
    factors = (factor_a, factor_b, factor_c, factor_d)

    def score(block, pair, slot):
        keys = both_sides(pair, 0)
        keys = jnp.concatenate([keys, keys], axis=1)
        scores[slot][...] = lax.dot_general(
            q_rows[rows_of(block)],
            keys,
            (((1,), (1,)), ((), ())),
            preferred_element_type=jnp.float32,
        )

    def weigh(block, shard, pair, slot):
        rows = rows_of(block)
        groups = groups_of(pair)
        seen = [mask[shard, at * 2 + half] > 0 for at, half in groups]
        parts = [scores[slot][:, n * 2 * HD : (n + 1) * 2 * HD] for n in range(len(groups))]
        best = None
        for part, ok in zip(parts, seen):
            most = jnp.where(ok, jnp.maximum(part[:, :HD], part[:, HD:]), NEG)
            best = most if best is None else jnp.maximum(best, most)
        old = top[rows]
        new = jnp.maximum(old, jnp.max(best, axis=1, keepdims=True))
        top[rows] = new
        for n, (part, ok) in enumerate(zip(parts, seen)):
            weights[slot][:, n * 2 * HD : (n + 1) * 2 * HD] = jnp.exp2(
                part - jnp.where(ok, new, BIG)
            ).astype(jnp.bfloat16)
        factors[slot][...] = jnp.exp2(old - new)

    def gather(block, pair, slot):
        rows = rows_of(block)
        values = both_sides(pair, 1)
        values = jnp.concatenate([values, jnp.ones_like(values)], axis=1)
        acc[rows] = acc[rows] * factors[slot][...] + jnp.dot(
            weights[slot][...], values, preferred_element_type=jnp.float32
        )

    def shard_at(step):
        return ((y + step) % 4) // 2

    def far_copy(phase, block):
        src = att_out.at[block]
        dst = att.at[phase, pl.ds(pl.multiple_of(core * BLOCK, BLOCK), BLOCK)]
        return remote(
            src, dst, a_send.at[phase, 0], a_recv.at[phase, core], in_column(2, y_hi)
        )

    def near_copy(phase, block, stays):
        src = att_out.at[block]
        dst = att.at[phase, pl.ds(pl.multiple_of(core * BLOCK, BLOCK), BLOCK)]
        if stays:
            return pltpu.make_async_copy(src, dst, a_recv.at[phase, core])
        return remote(src, dst, a_send.at[phase, 1], a_recv.at[phase, core], sibling)

    def normalise(block):
        rows = rows_of(block)
        attended = (acc[rows, :HD] / acc[rows, HD:]).astype(jnp.bfloat16)
        for one in range(SHARE):
            att_out[block, :, one * HD : (one + 1) * HD] = attended[one * BLOCK : (one + 1) * BLOCK]

    def send_far(phase):
        normalise(2 * phase)
        far_copy(phase, 2 * phase).start()

    def send_near(phase):
        normalise(2 * phase + 1)

        @pl.when(core == y_hi)
        def _():
            near_copy(phase, 2 * phase + 1, True).start()

        @pl.when(core != y_hi)
        def _():
            near_copy(phase, 2 * phase + 1, False).start()

    def part_copy(phase, n):
        return remote(
            part_out.at[phase, n],
            part_in.at[phase, n],
            p_send.at[phase, n],
            p_recv.at[phase, n],
            sibling,
        )

    def cross_copy(n):
        return remote(
            cross_out.at[n],
            cross_in.at[n],
            c_send.at[n],
            c_recv.at[n],
            in_column(3 - 2 * core, core),
        )

    def cross_send(n):
        part_copy(0, n).wait_recv()
        total = part_keep[n] + part_in[0, n].astype(jnp.float32)
        cross_out[n] = total.astype(jnp.bfloat16)
        cross_copy(n).start()

    def out_copy(n):
        columns = pl.ds(n * CHUNK, CHUNK)
        return pltpu.make_async_copy(res_here.at[:, columns], out.at[:, columns], o_sem.at[n])

    level = noise_level[span_here[0] * (1 - y_hi) + span_here[1] * y_hi]

    def finish(n):
        columns = slice(n * CHUNK, (n + 1) * CHUNK)
        gate = jnp.zeros((1, CHUNK), jnp.float32)
        for at in range(gate_here.shape[0]):
            gate = jnp.where(level == at, gate_here[at : at + 1, columns], gate)
        part_copy(1, n).wait_recv()
        cross_copy(n).wait_recv()
        total = part_keep[n] + part_in[1, n].astype(jnp.float32) + cross_in[n].astype(jnp.float32)
        res_here[:, columns] = (res_here[:, columns].astype(jnp.float32) + gate * total).astype(
            jnp.bfloat16
        )
        out_copy(n).start()

    def project(phase, use):
        for side in range(2):
            spot = att.at[phase, side * BLOCK : (side + 1) * BLOCK]
            remote(spot, spot, a_send.at[phase, 0], a_recv.at[phase, side], sibling).wait_recv()
        rows = att[phase]
        for n in range(CHUNKS + LAG):
            if n < CHUNKS:
                part = jnp.dot(
                    rows,
                    w_here[:, n * CHUNK : (n + 1) * CHUNK],
                    preferred_element_type=jnp.float32,
                )
                first, second = part[:BLOCK], part[BLOCK:]
                part_out[phase, n] = jnp.where(core == 0, second, first).astype(jnp.bfloat16)
                part_copy(phase, n).start()
                part_keep[n] = jnp.where(core == 0, first, second)
            if n >= LAG:
                use(n - LAG)

    query_copy(0).wait()
    take_queries(3)
    query_copy(1).wait_recv()
    query_copy(3).wait_recv()
    take_queries(0)
    take_queries(1)
    query_copy(2).wait_recv()
    take_queries(2)
    for offset in FIRST:
        arrive(*offset)
    side_wait(0)
    side_wait(1)
    score(0, 0, 0)
    last = STEPS - 1

    def ahead(pair, carry):
        for block in (2, 3):
            score(block, pair, block)
        for block in (2, 3):
            weigh(block, shard_at(6 - 2 * block), pair, block)
        for block in (2, 3):
            gather(block, pair, block)
        return carry

    def early(i, carry):
        for at, (low, high) in FILL.items():

            @pl.when(i == at)
            def _(low=low, high=high):
                lax.fori_loop(low, high, ahead, 0)

        for at in ARRIVE:

            @pl.when(i == at)
            def _(at=at):
                for offset in ARRIVE[at]:
                    arrive(*offset)

        gather(1, jnp.maximum(i - 1, 0), 1)
        score(1, i, 1)
        weigh(0, shard_at(1 + 2 * core), i, 0)
        for at in MIDDLE:

            @pl.when(i == at)
            def _(at=at):
                for offset in MIDDLE[at]:
                    arrive(*offset)

        @pl.when(i < last)
        def _():
            side_wait(2 * i + 2)
            side_wait(2 * i + 3)

        gather(0, i, 0)
        score(jnp.where(i == last, 2, 0), jnp.where(i == last, AHEAD, i + 1), 0)
        weigh(1, shard_at(3 - 2 * core), i, 1)
        return carry

    lax.fori_loop(0, STEPS, early, 0)
    send_far(0)
    local[0].wait()

    def block_of(n):
        return 2 + n // LEFT

    def pair_of(n):
        return AHEAD + n % LEFT

    def late(i, carry):
        n = 2 * i
        gather(
            jnp.where(i == 0, 1, block_of(jnp.maximum(n - 1, 0))),
            jnp.where(i == 0, last, pair_of(jnp.maximum(n - 1, 0))),
            1,
        )
        score(block_of(n + 1), pair_of(n + 1), 1)
        weigh(block_of(n), shard_at(6 - 2 * block_of(n)), pair_of(n), 0)
        gather(block_of(n), pair_of(n), 0)
        score(jnp.minimum(block_of(n + 2), 3), pair_of(n + 2), 0)
        weigh(block_of(n + 1), shard_at(6 - 2 * block_of(n + 1)), pair_of(n + 1), 1)

        @pl.when(i == 0)
        def _():
            send_near(0)

        @pl.when(i == LEFT // 2)
        def _():
            send_far(1)
            project(0, cross_send)

        return carry

    lax.fori_loop(0, LEFT, late, 0)
    gather(3, last, 1)
    send_near(1)
    local[1].wait()
    local[2].wait()
    project(1, finish)
    for n in range(CHUNKS):
        out_copy(n).wait()

    for step in (1, 2, 3):
        key_copy(step, 0).wait_send()
        key_copy(step, 1).wait_send()
        query_copy(step).wait_send()
    for first in range(4):
        for second in range(4):
            for copy in onward(first, second):
                copy.wait_send()
            side_copy(place(first, second)).wait_send()
    for phase in range(2):
        far_copy(phase, 2 * phase).wait_send()

        @pl.when(core != y_hi)
        def _(phase=phase):
            near_copy(phase, 2 * phase + 1, False).wait_send()

        for n in range(CHUNKS):
            part_copy(phase, n).wait_send()
    for n in range(CHUNKS):
        cross_copy(n).wait_send()


def copy_kernel(src, dst):
    dst[...] = src[...]


def on_device(*arrays):
    anywhere = pl.BlockSpec(memory_space=pl.ANY)
    scalars = pl.BlockSpec(memory_space=pltpu.SMEM)
    bf16, f32 = jnp.bfloat16, jnp.float32
    dma = pltpu.SemaphoreType.DMA
    mixed = pl.pallas_call(
        layer_kernel,
        out_shape=jax.ShapeDtypeStruct((BLOCK, D), bf16),
        in_specs=[anywhere] * 6 + [scalars] * 3,
        out_specs=anywhere,
        scratch_shapes=[
            pltpu.VMEM((COLUMNS, 2, 2, 2, HD, HD), bf16),
            pltpu.VMEM((4, BLOCK, WIDTH), bf16),
            pltpu.VMEM((4 * ROWS, 2 * HD), bf16),
            pltpu.VMEM((4 * ROWS, 1), f32),
            pltpu.VMEM((4 * ROWS, 2 * HD), f32),
            pltpu.VMEM((ROWS, 8 * HD), f32),
            pltpu.VMEM((ROWS, 8 * HD), f32),
            pltpu.VMEM((ROWS, 8 * HD), bf16),
            pltpu.VMEM((ROWS, 8 * HD), bf16),
            pltpu.VMEM((ROWS, 1), f32),
            pltpu.VMEM((ROWS, 1), f32),
            pltpu.VMEM((ROWS, 8 * HD), f32),
            pltpu.VMEM((ROWS, 8 * HD), f32),
            pltpu.VMEM((ROWS, 8 * HD), bf16),
            pltpu.VMEM((ROWS, 8 * HD), bf16),
            pltpu.VMEM((ROWS, 1), f32),
            pltpu.VMEM((ROWS, 1), f32),
            pltpu.VMEM((4, BLOCK, WIDTH), bf16),
            pltpu.VMEM((2, 2 * BLOCK, WIDTH), bf16),
            pltpu.VMEM((WIDTH, D), bf16),
            pltpu.VMEM((BLOCK, D), bf16),
            pltpu.VMEM((4, D), f32),
            pltpu.VMEM((2, CHUNKS, BLOCK, CHUNK), bf16),
            pltpu.VMEM((2, CHUNKS, BLOCK, CHUNK), bf16),
            pltpu.VMEM((CHUNKS, BLOCK, CHUNK), f32),
            pltpu.VMEM((CHUNKS, BLOCK, CHUNK), bf16),
            pltpu.VMEM((CHUNKS, BLOCK, CHUNK), bf16),
            pltpu.SMEM((2, 2 * COLUMNS), jnp.int32),
            pltpu.VMEM((BLOCK, KV_HEADS * WIDTH), bf16),
            pltpu.VMEM((BLOCK, KV_HEADS * HD), bf16),
            pltpu.VMEM((BLOCK, KV_HEADS * HD), bf16),
            dma((6,)),
            dma((4,)),
            dma((4,)),
            dma((4,)),
            dma((4,)),
            dma((4,)),
            dma((4,)),
            dma((COLUMNS, 2)),
            dma((COLUMNS, 2)),
            dma((COLUMNS,)),
            dma((COLUMNS,)),
            dma((2, 2)),
            dma((2, 2)),
            dma((2, CHUNKS)),
            dma((2, CHUNKS)),
            dma((CHUNKS,)),
            dma((CHUNKS,)),
            dma((CHUNKS,)),
        ],
        compiler_params=pltpu.CompilerParams(
            collective_id=0, has_side_effects=True, vmem_limit_bytes=58 * 2**20
        ),
        name="span_attention_layer",
    )(*arrays)
    return pl.pallas_call(
        copy_kernel,
        grid=(2,),
        out_shape=jax.ShapeDtypeStruct((BLOCK, D), bf16),
        in_specs=[pl.BlockSpec((BLOCK, D // 2), lambda i: (0, i))],
        out_specs=pl.BlockSpec((BLOCK, D // 2), lambda i: (0, i)),
        name="result",
    )(mixed)


def solution(mesh):
    tokens = P(("ctx", "head"), None)
    placed = (tokens, tokens, tokens, tokens, P("head", None), P(), P(), P(), P())
    return jax.shard_map(
        on_device, mesh=mesh, in_specs=placed, out_specs=tokens, check_vma=False
    )
```

```python
import math

import jax
import jax.numpy as jnp
from jax import lax
from jax.experimental import pallas as pl
from jax.experimental.pallas import tpu as pltpu
from jax.sharding import PartitionSpec as P

HD = 128
KV_HEADS = 4
SHARE = 6
WIDTH = SHARE * HD
BLOCK = 64
ROWS = SHARE * BLOCK
D = 6144
CHUNKS = 6
CHUNK = D // CHUNKS
RING = 4
NEG = -1e30
BIG = 1e30
MESH = pl.DeviceIdType.MESH

PLACE = {
    (0, 0): 0,
    (1, 0): 1,
    (0, 1): 2,
    (3, 0): 3,
    (0, 3): 4,
    (1, 1): 5,
    (3, 3): 6,
    (3, 1): 7,
    (1, 3): 8,
    (2, 0): 9,
    (0, 2): 10,
    (2, 1): 11,
    (1, 2): 12,
    (2, 3): 13,
    (3, 2): 14,
    (2, 2): 15,
}
COLUMNS = len(PLACE)
STEPS = COLUMNS // 2
FILL = {0: (0, 1), 1: (1, 2)}
AHEAD = 2
LEFT = STEPS - AHEAD
LAG = 4
FIRST = [(1, 0), (3, 0), (2, 0), (0, 1), (0, 3)]
ARRIVE = {1: [(1, 1), (3, 3), (3, 1), (1, 3), (2, 1), (2, 3), (0, 2)], 4: [(1, 2), (3, 2), (2, 2)]}
MIDDLE = {}


def layer_kernel(
    query,
    key,
    value,
    residual,
    weight,
    gate_table,
    span_of_shard,
    noise_level,
    visible,
    out,
    kv,
    q_in,
    q_rows,
    top,
    acc,
    score_a,
    score_b,
    weight_a,
    weight_b,
    factor_a,
    factor_b,
    score_c,
    score_d,
    weight_c,
    weight_d,
    factor_c,
    factor_d,
    att_out,
    att,
    w_here,
    res_here,
    gate_here,
    part_out,
    part_in,
    part_keep,
    cross_out,
    cross_in,
    mask,
    q_own,
    k_own,
    v_own,
    local_sem,
    k_send,
    k_recv,
    v_send,
    v_recv,
    q_send,
    q_recv,
    g_send,
    g_recv,
    s_send,
    s_recv,
    a_send,
    a_recv,
    p_send,
    p_recv,
    c_send,
    c_recv,
    o_sem,
):
    ctx = lax.axis_index("ctx")
    head = lax.axis_index("head")
    y_hi, x, z = ctx // 16, (ctx // 4) % 4, ctx % 4
    y_lo, core = head // 2, head % 2
    y = y_hi * 2 + y_lo
    other = 1 - core

    def device(y_at, x_at, z_at, core_at):
        return ((y_at // 2) * 16 + x_at * 4 + z_at, (y_at % 2) * 2 + core_at)

    def in_column(step, core_at):
        return device((y + step) % 4, x, z, core_at)

    sibling = in_column(0, other)

    def along(axis, step):
        on_x = (1 - core) if axis == 0 else core
        return device(y, (x + on_x * (step + 4)) % 4, (z + (1 - on_x) * (step + 4)) % 4, core)

    def place(first, second):
        a, b = PLACE[(first, second)], PLACE[(second, first)]
        return a if a == b else a + core * (b - a)

    def remote(src, dst, send, recv, to):
        return pltpu.make_async_remote_copy(
            src_ref=src, dst_ref=dst, send_sem=send, recv_sem=recv, device_id=to, device_id_type=MESH
        )

    local = [
        pltpu.make_async_copy(weight, w_here, local_sem.at[0]),
        pltpu.make_async_copy(residual, res_here, local_sem.at[1]),
        pltpu.make_async_copy(gate_table, gate_here, local_sem.at[2]),
    ]

    own = [
        pltpu.make_async_copy(key, k_own, local_sem.at[3]),
        pltpu.make_async_copy(value, v_own, local_sem.at[4]),
        pltpu.make_async_copy(query, q_own, local_sem.at[5]),
    ]
    for copy in own:
        copy.start()

    barrier = pltpu.get_barrier_semaphore()
    peers = [in_column(1, core), in_column(2, core), in_column(3, core)]
    peers += [sibling, in_column(2, other)]
    peers += [along(0, 1), along(0, -1), along(1, 1), along(1, -1), along(0, 2), along(1, 2)]
    for peer in peers:
        pl.semaphore_signal(barrier, inc=1, device_id=peer, device_id_type=MESH)
    top[...] = jnp.full(top.shape, NEG, jnp.float32)
    acc[...] = jnp.zeros(acc.shape, jnp.float32)
    for copy in own:
        copy.wait()
    pl.semaphore_wait(barrier, len(peers))

    key_rows = pl.ds(pl.multiple_of(y_lo * BLOCK, BLOCK), BLOCK)

    def key_copy(step, which):
        chip = (y + step) % 4
        group = (chip % 2) * 2 + chip // 2
        src = (k_own, v_own)[which].at[:, pl.ds(pl.multiple_of(group * HD, HD), HD)]
        dst = kv.at[0, core, y_hi, which, key_rows]
        send, recv = ((k_send, k_recv), (v_send, v_recv))[which]
        if step == 0:
            return pltpu.make_async_copy(src, dst, recv.at[0])
        return remote(src, dst, send.at[step], recv.at[step], in_column(step, core))

    def query_copy(step):
        chip = (y + step) % 4
        group = (chip % 2) * 2 + chip // 2
        src = q_own.at[:, pl.ds(pl.multiple_of(group * WIDTH, WIDTH), WIDTH)]
        block = {0: 3, 1: 1 - core, 2: 2, 3: core}[step]
        dst = q_in.at[block]
        if step == 0:
            return pltpu.make_async_copy(src, dst, q_recv.at[0])
        return remote(src, dst, q_send.at[step], q_recv.at[step], in_column(step, core))

    for step in (2, 1, 3, 0):
        for which in range(2):
            key_copy(step, which).start()
    for step in (1, 3, 2, 0):
        query_copy(step).start()
    for copy in local:
        copy.start()

    span_here = [span_of_shard[x * 4 + z], span_of_shard[16 + x * 4 + z]]
    for (dx, dz), at in PLACE.items():
        column = ((x + 4 - dx) % 4) * 4 + (z + 4 - dz) % 4
        for half in range(2):
            span = span_of_shard[half * 16 + column]
            for row in range(2):
                mask[row, at * 2 + half] = visible[span_here[row], span]

    def ring_copy(first, second, axis, step, half):
        there = ((first + step) % 4, second) if axis == 0 else (first, (second + step) % 4)
        at = place(*there)
        if half is None:
            src, dst, n = kv.at[place(first, second), core], kv.at[at, core], 0
        else:
            src, dst, n = kv.at[place(first, second), core, half], kv.at[at, core, half], half
        return remote(src, dst, g_send.at[at, n], g_recv.at[at, n], along(axis, step))

    def side_copy(at):
        return remote(kv.at[at, core], kv.at[at, core], s_send.at[at], s_recv.at[at], sibling)

    def side_wait(at):
        remote(kv.at[at, other], kv.at[at, other], s_send.at[at], s_recv.at[at], sibling).wait_recv()

    def onward(first, second):
        ways = []
        if second == 0:
            if first == 0:
                ways += [(0, 1, None), (0, -1, None), (0, 2, None)]
            ways += [(1, 1, None), (1, -1, None)]
        elif second == 1:
            ways += [(1, 1, 0)]
        elif second == 3:
            ways += [(1, -1, 1)]
        return [ring_copy(first, second, *way) for way in ways]

    def arrive(first, second):
        at = place(first, second)
        if second == 2:
            for half in range(2):
                spot = kv.at[at, core, half]
                remote(spot, spot, g_send.at[at, half], g_recv.at[at, half], sibling).wait_recv()
        else:
            spot = kv.at[at, core]
            remote(spot, spot, g_send.at[at, 0], g_recv.at[at, 0], sibling).wait_recv()
        for copy in onward(first, second):
            copy.start()
        side_copy(at).start()

    for step in range(4):
        for which in range(2):
            copy = key_copy(step, which)
            if step == 0:
                copy.wait()
            else:
                copy.wait_recv()
    for copy in onward(0, 0):
        copy.start()
    side_copy(0).start()
    weight_a[...] = jnp.zeros(weight_a.shape, jnp.bfloat16)
    weight_b[...] = jnp.zeros(weight_b.shape, jnp.bfloat16)
    factor_a[...] = jnp.ones(factor_a.shape, jnp.float32)
    factor_b[...] = jnp.ones(factor_b.shape, jnp.float32)
    scale = math.log2(math.e) / math.sqrt(HD)

    def take_queries(block):
        for one in range(SHARE):
            rows = q_in[block, :, one * HD : (one + 1) * HD].astype(jnp.float32) * scale
            upper = rows.astype(jnp.bfloat16)
            lower = (rows - upper.astype(jnp.float32)).astype(jnp.bfloat16)
            spot = pl.ds(block * ROWS + one * BLOCK, BLOCK)
            q_rows[spot, :HD] = upper
            q_rows[spot, HD:] = lower

    def rows_of(block):
        if isinstance(block, int):
            return pl.ds(block * ROWS, ROWS)
        return pl.ds(pl.multiple_of(block * ROWS, ROWS), ROWS)

    def groups_of(pair):
        return [(2 * pair + late, half) for late in range(2) for half in range(2)]

    def both_sides(pair, which):
        return jnp.concatenate(
            [kv[at, side, half, which] for at, half in groups_of(pair) for side in range(2)], axis=0
        )

    scores = (score_a, score_b, score_c, score_d)
    weights = (weight_a, weight_b, weight_c, weight_d)
    factors = (factor_a, factor_b, factor_c, factor_d)

    def score(block, pair, slot):
        keys = both_sides(pair, 0)
        keys = jnp.concatenate([keys, keys], axis=1)
        scores[slot][...] = lax.dot_general(
            q_rows[rows_of(block)],
            keys,
            (((1,), (1,)), ((), ())),
            preferred_element_type=jnp.float32,
        )

    def weigh(block, shard, pair, slot):
        rows = rows_of(block)
        groups = groups_of(pair)
        seen = [mask[shard, at * 2 + half] > 0 for at, half in groups]
        parts = [scores[slot][:, n * 2 * HD : (n + 1) * 2 * HD] for n in range(len(groups))]
        best = None
        for part, ok in zip(parts, seen):
            most = jnp.where(ok, jnp.maximum(part[:, :HD], part[:, HD:]), NEG)
            best = most if best is None else jnp.maximum(best, most)
        old = top[rows]
        new = jnp.maximum(old, jnp.max(best, axis=1, keepdims=True))
        top[rows] = new
        for n, (part, ok) in enumerate(zip(parts, seen)):
            weights[slot][:, n * 2 * HD : (n + 1) * 2 * HD] = jnp.exp2(
                part - jnp.where(ok, new, BIG)
            ).astype(jnp.bfloat16)
        factors[slot][...] = jnp.exp2(old - new)

    def gather(block, pair, slot):
        rows = rows_of(block)
        values = both_sides(pair, 1)
        values = jnp.concatenate([values, jnp.ones_like(values)], axis=1)
        acc[rows] = acc[rows] * factors[slot][...] + jnp.dot(
            weights[slot][...], values, preferred_element_type=jnp.float32
        )

    def shard_at(step):
        return ((y + step) % 4) // 2

    def far_copy(phase, block):
        src = att_out.at[block]
        dst = att.at[phase, pl.ds(pl.multiple_of(core * BLOCK, BLOCK), BLOCK)]
        return remote(
            src, dst, a_send.at[phase, 0], a_recv.at[phase, core], in_column(2, y_hi)
        )

    def near_copy(phase, block, stays):
        src = att_out.at[block]
        dst = att.at[phase, pl.ds(pl.multiple_of(core * BLOCK, BLOCK), BLOCK)]
        if stays:
            return pltpu.make_async_copy(src, dst, a_recv.at[phase, core])
        return remote(src, dst, a_send.at[phase, 1], a_recv.at[phase, core], sibling)

    def normalise(block):
        rows = rows_of(block)
        attended = (acc[rows, :HD] / acc[rows, HD:]).astype(jnp.bfloat16)
        for one in range(SHARE):
            att_out[block, :, one * HD : (one + 1) * HD] = attended[one * BLOCK : (one + 1) * BLOCK]

    def send_far(phase):
        normalise(2 * phase)
        far_copy(phase, 2 * phase).start()

    def send_near(phase):
        normalise(2 * phase + 1)

        @pl.when(core == y_hi)
        def _():
            near_copy(phase, 2 * phase + 1, True).start()

        @pl.when(core != y_hi)
        def _():
            near_copy(phase, 2 * phase + 1, False).start()

    def part_copy(phase, n):
        return remote(
            part_out.at[phase, n],
            part_in.at[phase, n],
            p_send.at[phase, n],
            p_recv.at[phase, n],
            sibling,
        )

    def cross_copy(n):
        return remote(
            cross_out.at[n],
            cross_in.at[n],
            c_send.at[n],
            c_recv.at[n],
            in_column(3 - 2 * core, core),
        )

    def cross_send(n):
        part_copy(0, n).wait_recv()
        total = part_keep[n] + part_in[0, n].astype(jnp.float32)
        cross_out[n] = total.astype(jnp.bfloat16)
        cross_copy(n).start()

    def out_copy(n):
        columns = pl.ds(n * CHUNK, CHUNK)
        return pltpu.make_async_copy(res_here.at[:, columns], out.at[:, columns], o_sem.at[n])

    level = noise_level[span_here[0] * (1 - y_hi) + span_here[1] * y_hi]

    def finish(n):
        columns = slice(n * CHUNK, (n + 1) * CHUNK)
        gate = jnp.zeros((1, CHUNK), jnp.float32)
        for at in range(gate_here.shape[0]):
            gate = jnp.where(level == at, gate_here[at : at + 1, columns], gate)
        part_copy(1, n).wait_recv()
        cross_copy(n).wait_recv()
        total = part_keep[n] + part_in[1, n].astype(jnp.float32) + cross_in[n].astype(jnp.float32)
        res_here[:, columns] = (res_here[:, columns].astype(jnp.float32) + gate * total).astype(
            jnp.bfloat16
        )
        out_copy(n).start()

    def project(phase, use):
        for side in range(2):
            spot = att.at[phase, side * BLOCK : (side + 1) * BLOCK]
            remote(spot, spot, a_send.at[phase, 0], a_recv.at[phase, side], sibling).wait_recv()
        rows = att[phase]
        for n in range(CHUNKS + LAG):
            if n < CHUNKS:
                part = jnp.dot(
                    rows,
                    w_here[:, n * CHUNK : (n + 1) * CHUNK],
                    preferred_element_type=jnp.float32,
                )
                first, second = part[:BLOCK], part[BLOCK:]
                part_out[phase, n] = jnp.where(core == 0, second, first).astype(jnp.bfloat16)
                part_copy(phase, n).start()
                part_keep[n] = jnp.where(core == 0, first, second)
            if n >= LAG:
                use(n - LAG)

    query_copy(0).wait()
    take_queries(3)
    query_copy(1).wait_recv()
    query_copy(3).wait_recv()
    take_queries(0)
    take_queries(1)
    query_copy(2).wait_recv()
    take_queries(2)
    for offset in FIRST:
        arrive(*offset)
    side_wait(0)
    side_wait(1)
    score(0, 0, 0)
    last = STEPS - 1

    def ahead(pair, carry):
        for block in (2, 3):
            score(block, pair, block)
        for block in (2, 3):
            weigh(block, shard_at(6 - 2 * block), pair, block)
        for block in (2, 3):
            gather(block, pair, block)
        return carry

    def early(i, carry):
        for at, (low, high) in FILL.items():

            @pl.when(i == at)
            def _(low=low, high=high):
                lax.fori_loop(low, high, ahead, 0)

        for at in ARRIVE:

            @pl.when(i == at)
            def _(at=at):
                for offset in ARRIVE[at]:
                    arrive(*offset)

        gather(1, jnp.maximum(i - 1, 0), 1)
        score(1, i, 1)
        weigh(0, shard_at(1 + 2 * core), i, 0)
        for at in MIDDLE:

            @pl.when(i == at)
            def _(at=at):
                for offset in MIDDLE[at]:
                    arrive(*offset)

        @pl.when(i < last)
        def _():
            side_wait(2 * i + 2)
            side_wait(2 * i + 3)

        gather(0, i, 0)
        score(jnp.where(i == last, 2, 0), jnp.where(i == last, AHEAD, i + 1), 0)
        weigh(1, shard_at(3 - 2 * core), i, 1)
        return carry

    lax.fori_loop(0, STEPS, early, 0)
    send_far(0)
    local[0].wait()

    def block_of(n):
        return 2 + n // LEFT

    def pair_of(n):
        return AHEAD + n % LEFT

    def late(i, carry):
        n = 2 * i
        gather(
            jnp.where(i == 0, 1, block_of(jnp.maximum(n - 1, 0))),
            jnp.where(i == 0, last, pair_of(jnp.maximum(n - 1, 0))),
            1,
        )
        score(block_of(n + 1), pair_of(n + 1), 1)
        weigh(block_of(n), shard_at(6 - 2 * block_of(n)), pair_of(n), 0)
        gather(block_of(n), pair_of(n), 0)
        score(jnp.minimum(block_of(n + 2), 3), pair_of(n + 2), 0)
        weigh(block_of(n + 1), shard_at(6 - 2 * block_of(n + 1)), pair_of(n + 1), 1)

        @pl.when(i == 0)
        def _():
            send_near(0)

        @pl.when(i == LEFT // 2)
        def _():
            send_far(1)
            project(0, cross_send)

        return carry

    lax.fori_loop(0, LEFT, late, 0)
    gather(3, last, 1)
    send_near(1)
    local[1].wait()
    local[2].wait()
    project(1, finish)
    for n in range(CHUNKS):
        out_copy(n).wait()

    for step in (1, 2, 3):
        key_copy(step, 0).wait_send()
        key_copy(step, 1).wait_send()
        query_copy(step).wait_send()
    for first in range(4):
        for second in range(4):
            for copy in onward(first, second):
                copy.wait_send()
            side_copy(place(first, second)).wait_send()
    for phase in range(2):
        far_copy(phase, 2 * phase).wait_send()

        @pl.when(core != y_hi)
        def _(phase=phase):
            near_copy(phase, 2 * phase + 1, False).wait_send()

        for n in range(CHUNKS):
            part_copy(phase, n).wait_send()
    for n in range(CHUNKS):
        cross_copy(n).wait_send()


def copy_kernel(src, dst):
    dst[...] = src[...]


def on_device(*arrays):
    anywhere = pl.BlockSpec(memory_space=pl.ANY)
    scalars = pl.BlockSpec(memory_space=pltpu.SMEM)
    bf16, f32 = jnp.bfloat16, jnp.float32
    dma = pltpu.SemaphoreType.DMA
    mixed = pl.pallas_call(
        layer_kernel,
        out_shape=jax.ShapeDtypeStruct((BLOCK, D), bf16),
        in_specs=[anywhere] * 6 + [scalars] * 3,
        out_specs=anywhere,
        scratch_shapes=[
            pltpu.VMEM((COLUMNS, 2, 2, 2, HD, HD), bf16),
            pltpu.VMEM((4, BLOCK, WIDTH), bf16),
            pltpu.VMEM((4 * ROWS, 2 * HD), bf16),
            pltpu.VMEM((4 * ROWS, 1), f32),
            pltpu.VMEM((4 * ROWS, 2 * HD), f32),
            pltpu.VMEM((ROWS, 8 * HD), f32),
            pltpu.VMEM((ROWS, 8 * HD), f32),
            pltpu.VMEM((ROWS, 8 * HD), bf16),
            pltpu.VMEM((ROWS, 8 * HD), bf16),
            pltpu.VMEM((ROWS, 1), f32),
            pltpu.VMEM((ROWS, 1), f32),
            pltpu.VMEM((ROWS, 8 * HD), f32),
            pltpu.VMEM((ROWS, 8 * HD), f32),
            pltpu.VMEM((ROWS, 8 * HD), bf16),
            pltpu.VMEM((ROWS, 8 * HD), bf16),
            pltpu.VMEM((ROWS, 1), f32),
            pltpu.VMEM((ROWS, 1), f32),
            pltpu.VMEM((4, BLOCK, WIDTH), bf16),
            pltpu.VMEM((2, 2 * BLOCK, WIDTH), bf16),
            pltpu.VMEM((WIDTH, D), bf16),
            pltpu.VMEM((BLOCK, D), bf16),
            pltpu.VMEM((4, D), f32),
            pltpu.VMEM((2, CHUNKS, BLOCK, CHUNK), bf16),
            pltpu.VMEM((2, CHUNKS, BLOCK, CHUNK), bf16),
            pltpu.VMEM((CHUNKS, BLOCK, CHUNK), f32),
            pltpu.VMEM((CHUNKS, BLOCK, CHUNK), bf16),
            pltpu.VMEM((CHUNKS, BLOCK, CHUNK), bf16),
            pltpu.SMEM((2, 2 * COLUMNS), jnp.int32),
            pltpu.VMEM((BLOCK, KV_HEADS * WIDTH), bf16),
            pltpu.VMEM((BLOCK, KV_HEADS * HD), bf16),
            pltpu.VMEM((BLOCK, KV_HEADS * HD), bf16),
            dma((6,)),
            dma((4,)),
            dma((4,)),
            dma((4,)),
            dma((4,)),
            dma((4,)),
            dma((4,)),
            dma((COLUMNS, 2)),
            dma((COLUMNS, 2)),
            dma((COLUMNS,)),
            dma((COLUMNS,)),
            dma((2, 2)),
            dma((2, 2)),
            dma((2, CHUNKS)),
            dma((2, CHUNKS)),
            dma((CHUNKS,)),
            dma((CHUNKS,)),
            dma((CHUNKS,)),
        ],
        compiler_params=pltpu.CompilerParams(
            collective_id=0, has_side_effects=True, vmem_limit_bytes=58 * 2**20
        ),
        name="span_attention_layer",
    )(*arrays)
    return pl.pallas_call(
        copy_kernel,
        grid=(2,),
        out_shape=jax.ShapeDtypeStruct((BLOCK, D), bf16),
        in_specs=[pl.BlockSpec((BLOCK, D // 2), lambda i: (0, i))],
        out_specs=pl.BlockSpec((BLOCK, D // 2), lambda i: (0, i)),
        name="result",
    )(mixed)


def solution(mesh):
    tokens = P(("ctx", "head"), None)
    placed = (tokens, tokens, tokens, tokens, P("head", None), P(), P(), P(), P())
    return jax.shard_map(
        on_device, mesh=mesh, in_specs=placed, out_specs=tokens, check_vma=False
    )
```
